256 devices in a mesh: grp: 8 (over y, core), col: 32 (over x, z).
Axes of the slice: x: 4, y: 4, z: 8, core: 2. Of those that a mesh axis runs over, the one named last changes fastest.
Arguments:
- state: float32 [2, 64, 524288], P(None, None, ('grp', 'col')), may hold values from -6 to 6
- wind: float32 [2, 64, 524288], P(None, None, ('grp', 'col')), may hold values from -5 to 5
- live: int32 [8, 32], P('grp'), may hold values from 1 to 128, 2048 in all within a row
- w_first: bfloat16 [128, 1024], replicated, may hold values from -0.5 to 0.5
- b_first: float32 [1024], replicated, may hold values from -3 to 3
- w_second: bfloat16 [1024, 1024], replicated, may hold values from -0.1875 to 0.1875
- b_second: float32 [1024], replicated, may hold values from -3 to 3
- w_third: bfloat16 [1024, 128], replicated, may hold values from -0.1875 to 0.1875
- b_third: float32 [128], replicated, may hold values from -2 to 2
Outputs:
- updated: float32 [2, 64, 524288], P(None, None, ('grp', 'col'))
The draws below stay inside these ranges and needn't reach their ends.
Inputs may be any that keep to these rules, and one draw needn't show every extreme that they name: `live`: the 32 counts of each group sum to 2048, and in each group some device holds exactly 128.
All inputs are finite; a program needn't handle non-finite values.
Results may differ from the reference program's by a relative error of at most 0.0023.
Values may be sent and summed in bfloat16 or wider, within the bound.
No kernel may reach another device: no remote copies, remote signals or barrier semaphores. Data moves between devices by JAX's collectives and lax.ppermute only.
A program may use at most 64 MiB of HBM per device.

```python
import math
import jax
import jax.numpy as jnp
import numpy as np
from jax import lax

LEV = 64
UNITS = 1024
EMEAN = 64
COLS = 524288
N_GRP = 8
N_COL = 32


def levels(rng, shape, pieces, low, top_value):
    gain, own = 1.0, jax.random.fold_in(rng, 6)
    for position, parts in pieces:
        steps = jnp.exp(jax.random.uniform(jax.random.fold_in(own, position), (parts,), jnp.float32, low / len(pieces), top_value / len(pieces)))
        gain = gain * jnp.repeat(steps, shape[position] // parts).reshape([-1 if axis == position else 1 for axis in range(len(shape))])
    return gain


def profile(amount, total, bound, lean):
    weights = [(1 << 20) // math.isqrt(rank ** lean) + 1 for rank in range(2, amount + 1)]
    spare, given = total - bound - (amount - 1), [1] * (amount - 1)
    while spare > 0:
        free = [i for i in range(amount - 1) if given[i] < bound]
        pool, left = sum([weights[i] for i in free]), spare
        for i in free:
            extra = min(bound - given[i], max(1, left * weights[i] // pool), spare)
            given[i] = given[i] + extra
            spare = spare - extra
    return np.array([bound] + given)


def ragged_sizes(key, amount, total, reach, lean):
    if amount == 2:
        one = jax.random.randint(key, (), max(1, total - reach), min(reach, total - 1) + 1)
        return jnp.stack([one, total - one])
    lengths = jnp.asarray(profile(amount, total, reach, lean), jnp.int32)
    pairs = (amount - 1) // 2
    donor, receiver = lengths[1:1 + 2 * pairs:2], lengths[2:2 + 2 * pairs:2]
    room = jnp.minimum(donor - 1, reach - receiver)
    passed = jax.random.randint(jax.random.fold_in(key, 1), (pairs,), 0, 1 << 20) % (room + 1)
    lengths = lengths.at[1:1 + 2 * pairs:2].set(donor - passed).at[2:2 + 2 * pairs:2].set(receiver + passed)
    return lengths[jax.random.permutation(jax.random.fold_in(key, 2), amount)]


def scatter_about(stream_key, shape, scale, most, pieces=(), kind=jnp.bfloat16):
    factor_of = levels(stream_key, shape, pieces, -0.22, 0.18) if pieces else 1.0
    values = jax.random.normal(stream_key, shape, jnp.float32) * scale * factor_of
    return jnp.minimum(jnp.maximum(values, -most), most).astype(kind)


def setup_inputs(seed: int = 0) -> dict:
    key_of = jax.random.split(jax.random.key(seed), 10)
    state = scatter_about(key_of[0], (2, LEV, COLS), 1.0, 6.0, ((2, 256),), jnp.float32)
    wind = scatter_about(key_of[1], (2, LEV, COLS), 1.0, 5.0, ((2, 256),), jnp.float32)
    live = jax.vmap(lambda own: ragged_sizes(own, N_COL, N_COL * EMEAN, 2 * EMEAN, 2))(jax.random.split(key_of[2], N_GRP)).reshape((N_GRP, N_COL)).astype(jnp.int32)
    w_first = scatter_about(key_of[3], (2 * LEV, UNITS), (2 * LEV) ** -0.5, 0.5)
    b_first = scatter_about(key_of[4], (UNITS,), 0.5, 3.0, (), jnp.float32)
    w_second = scatter_about(key_of[5], (UNITS, UNITS), UNITS ** -0.5, 0.1875)
    b_second = scatter_about(key_of[6], (UNITS,), 0.5, 3.0, (), jnp.float32)
    w_third = scatter_about(key_of[7], (UNITS, 2 * LEV), UNITS ** -0.5, 0.1875)
    b_third = scatter_about(key_of[8], (2 * LEV,), 0.3, 2.0, (), jnp.float32)
    return {"state": state, "wind": wind, "live": live, "w_first": w_first, "b_first": b_first, "w_second": w_second, "b_second": b_second, "w_third": w_third, "b_third": b_third}


TIMESTEP = 0.1

def gll_table():
    points = np.array([-1.0, -1.0 / np.sqrt(5.0), 1.0 / np.sqrt(5.0), 1.0])
    legendre = 0.5 * (5.0 * points ** 3 - 3.0 * points)
    deriv_table = np.zeros((4, 4))
    for i in range(4):
        for j in range(4):
            if i != j:
                deriv_table[i, j] = legendre[i] / (legendre[j] * (points[i] - points[j]))
    deriv_table[0, 0] = -3.0
    deriv_table[3, 3] = 3.0
    return deriv_table

def physics_net(inputs, w_first, b_first, w_second, b_second, w_third, b_third):
    first = jnp.dot(inputs, w_first, preferred_element_type=jnp.float32) + b_first
    hidden = jax.nn.silu(first).astype(jnp.bfloat16)
    second = jnp.dot(hidden, w_second, preferred_element_type=jnp.float32) + b_second
    deeper = jax.nn.silu(second).astype(jnp.bfloat16)
    return (jnp.dot(deeper, w_third, preferred_element_type=jnp.float32) + b_third).astype(jnp.bfloat16)

def reference(state, wind, live, w_first, b_first, w_second, b_second, w_third, b_third):
    devices = N_GRP * N_COL
    columns = 32 * EMEAN
    fields = 2
    features = fields * LEV
    deriv_table = jnp.asarray(gll_table(), jnp.float32)
    element_grid = state.reshape(fields, LEV, devices, columns // 16, 4, 4)
    d_xi = jnp.einsum('ab,fldejb->fldeja', deriv_table, element_grid, precision=lax.Precision.HIGHEST).reshape(fields, LEV, devices, columns)
    d_eta = jnp.einsum('ab,fldebi->fldeai', deriv_table, element_grid, precision=lax.Precision.HIGHEST).reshape(fields, LEV, devices, columns)
    wind_field = wind.reshape(2, LEV, devices, columns)
    dyn_rate = -(wind_field[0][None] * d_xi + wind_field[1][None] * d_eta)
    counts = live.reshape(devices).astype(jnp.int32) * 16
    node_ids = jnp.arange(16, dtype=jnp.int32)
    last_index = (counts - 16)[:, None] + node_ids[None, :]
    last_elem = jnp.take_along_axis(dyn_rate, jnp.broadcast_to(last_index[None, None], (fields, LEV, devices, 16)), axis=3)
    before = jnp.roll(last_elem, 1, axis=2)
    after_elem = jnp.roll(dyn_rate[..., :16], -1, axis=2)
    padded = jnp.concatenate([before, dyn_rate, jnp.zeros_like(before)], axis=3)
    spot_ids = jnp.arange(columns + 32, dtype=jnp.int32)
    offset = spot_ids[None, :] - 16 - counts[:, None]
    inside = (offset >= 0) & (offset < 16)
    placed = jnp.take_along_axis(after_elem, jnp.broadcast_to(jnp.clip(offset, 0, 15)[None, None], (fields, LEV, devices, columns + 32)), axis=3)
    padded = jnp.where(inside[None, None], placed, padded)
    east_twin = padded[..., 29:29 + columns]
    west_twin = padded[..., 3:3 + columns]
    column_ids = jnp.arange(columns, dtype=jnp.int32)
    alive_mask = column_ids[None, :] < counts[:, None]
    east_mask = alive_mask & (column_ids % 4 == 3)[None, :]
    west_mask = alive_mask & (column_ids % 4 == 0)[None, :]
    summed = jnp.where(east_mask[None, None], 0.5 * (dyn_rate + east_twin), jnp.where(west_mask[None, None], 0.5 * (dyn_rate + west_twin), dyn_rate))
    column_rows = state.reshape(features, devices * columns).T.astype(jnp.bfloat16)
    live_picks = jnp.nonzero(alive_mask.reshape(devices * columns), size=devices * columns // 2)[0].astype(jnp.int32)
    chosen = column_rows[live_picks].reshape(devices, columns // 2, features)
    results = lax.map(lambda part: physics_net(part, w_first, b_first, w_second, b_second, w_third, b_third), chosen)
    tendency_rows = jnp.zeros((devices * columns, features), jnp.bfloat16).at[live_picks].set(results.reshape(devices * columns // 2, features))
    tendency = tendency_rows.astype(jnp.float32).T.reshape(fields, LEV, devices, columns)
    base = state.reshape(fields, LEV, devices, columns)
    updated = jnp.where(alive_mask[None, None], base + TIMESTEP * summed + tendency, jnp.float32(0.0))
    return updated.reshape(fields, LEV, devices * columns)
```

```python
import functools

import jax
import jax.numpy as jnp
import numpy as np
from jax import lax
from jax.experimental import pallas as pl
from jax.experimental.pallas import tpu as pltpu
from jax.sharding import PartitionSpec as P

TIMESTEP = 0.1
LANES = 128
TILE = 512
CHUNK = 256
BF = jnp.bfloat16
F32 = jnp.float32
MIB = 2**20


def gll_table():
    points = np.array([-1.0, -1.0 / np.sqrt(5.0), 1.0 / np.sqrt(5.0), 1.0])
    legendre = 0.5 * (5.0 * points**3 - 3.0 * points)
    deriv_table = np.zeros((4, 4))
    for i in range(4):
        for j in range(4):
            if i != j:
                deriv_table[i, j] = legendre[i] / (legendre[j] * (points[i] - points[j]))
    deriv_table[0, 0] = -3.0
    deriv_table[3, 3] = 3.0
    return deriv_table


def deriv_operand():
    deriv_table = gll_table()
    along_xi = np.kron(np.eye(8), np.kron(np.eye(4), deriv_table)).T
    along_eta = np.kron(np.eye(8), np.kron(deriv_table, np.eye(4))).T
    both = np.concatenate([along_xi, along_eta], axis=1).astype(np.float32)
    high = both.astype(jnp.bfloat16)
    low = (both - high.astype(np.float32)).astype(jnp.bfloat16)
    return jnp.asarray(np.concatenate([high, high, low], axis=0))


def block_rate(s, wind_xi, wind_eta, deriv):
    high = s.astype(BF)
    low = (s - high.astype(F32)).astype(BF)
    d = jnp.dot(
        jnp.concatenate([high, low, high], axis=1), deriv, preferred_element_type=F32
    )
    return -(wind_xi * d[:, :LANES] + wind_eta * d[:, LANES:])


def both_fields(w):
    return jnp.concatenate([w, w], axis=0)


def lane_ids():
    return lax.broadcasted_iota(jnp.int32, (LANES, LANES), 1)


def own_live(live_ref):
    return live_ref[0, lax.axis_index("col")] * 16


def edge_kernel(live_ref, s_hbm, w_hbm, d_hbm, last_ref, first_ref, s_v, w_v, deriv, sems):
    start = own_live(live_ref) - 16
    block = pl.multiple_of(start // LANES * LANES, LANES)
    copies = [
        pltpu.make_async_copy(s_hbm.at[:, pl.ds(0, LANES)], s_v.at[0], sems.at[0]),
        pltpu.make_async_copy(w_hbm.at[:, pl.ds(0, LANES)], w_v.at[0], sems.at[1]),
        pltpu.make_async_copy(s_hbm.at[:, pl.ds(block, LANES)], s_v.at[1], sems.at[2]),
        pltpu.make_async_copy(w_hbm.at[:, pl.ds(block, LANES)], w_v.at[1], sems.at[3]),
        pltpu.make_async_copy(d_hbm, deriv, sems.at[4]),
    ]
    for copy in copies:
        copy.start()
    for copy in copies:
        copy.wait()
    rates = [
        block_rate(s_v[k], both_fields(w_v[k, 0:64]), both_fields(w_v[k, 64:128]), deriv[...])
        for k in range(2)
    ]
    rows = lax.broadcasted_iota(jnp.int32, (16, LANES), 0)
    turn = LANES - 3 - (start - block)
    east = pltpu.roll(rates[1], jnp.where(turn < 0, turn + LANES, turn), 1).T[0:16]
    last_ref[...] = jnp.where(rows % 4 == 0, east, 0.0)
    west = pltpu.roll(rates[0], 3, 1).T[0:16]
    first_ref[...] = jnp.where(rows % 4 == 3, west, 0.0)


def main_kernel(
    live_ref, s_hbm, w_hbm, w1_hbm, b1_hbm, w2_hbm, b2_hbm, w3_hbm, b3_hbm, d_hbm, o_hbm,
    s_v, w_v, w1, b1, w2, b2, w3, b3, deriv, w3t, h1, h2, rate, o_v, in_sems, out_sems,
):
    columns, units = h1.shape
    tiles = columns // TILE
    count = own_live(live_ref)

    def fetch(index, source, target):
        copy = pltpu.make_async_copy(source, target, in_sems.at[index])
        copy.start()
        return copy

    def cut(ref, tile):
        return ref.at[:, pl.ds(tile * TILE, TILE)]

    s_copies = [fetch(0, cut(s_hbm, 0), cut(s_v, 0))]
    early = [fetch(4, w1_hbm, w1), fetch(5, b1_hbm, b1)]
    s_copies += [fetch(t, cut(s_hbm, t), cut(s_v, t)) for t in range(1, tiles)]
    later = [
        fetch(6, w2_hbm, w2),
        fetch(7, b2_hbm, b2),
        fetch(8, w3_hbm, w3),
        fetch(9, b3_hbm, b3),
        fetch(10, d_hbm, deriv),
        fetch(11, w_hbm, w_v),
    ]
    for copy in early:
        copy.wait()
    for t in range(tiles):
        s_copies[t].wait()
        x = s_v[:, t * TILE : (t + 1) * TILE].astype(BF)
        for n in range(0, units, CHUNK):
            a = lax.dot_general(
                x, w1[:, n : n + CHUNK], (((0,), (0,)), ((), ())), preferred_element_type=F32
            )
            h1[t * TILE : (t + 1) * TILE, n : n + CHUNK] = jax.nn.silu(
                a + b1[:, n : n + CHUNK]
            ).astype(BF)
    for copy in later:
        copy.wait()
    w3t[...] = w3[...].T
    b3_rows = jnp.broadcast_to(b3[...], (LANES, LANES)).T
    for c in range(0, columns, LANES):
        cols = slice(c, c + LANES)
        rate[:, cols] = block_rate(
            s_v[:, cols], both_fields(w_v[0:64, cols]), both_fields(w_v[64:128, cols]), deriv[...]
        )
    lanes = lane_ids()
    outs = []
    for t in range(tiles):
        rows = slice(t * TILE, (t + 1) * TILE)
        for n in range(0, units, CHUNK):
            a = jnp.dot(h1[rows], w2[:, n : n + CHUNK], preferred_element_type=F32)
            h2[rows, n : n + CHUNK] = jax.nn.silu(a + b2[:, n : n + CHUNK]).astype(BF)
        third = lax.dot_general(
            w3t[...], h2[rows], (((1,), (1,)), ((), ())), preferred_element_type=F32
        )
        for c in range(t * TILE, (t + 1) * TILE, LANES):
            cols = slice(c, c + LANES)
            own = rate[:, cols]
            after = rate[:, c + LANES : c + 2 * LANES] if c + LANES < columns else own
            prior = rate[:, c - LANES : c] if c else own
            ids = lanes + c
            east = jnp.where(
                lanes < LANES - 13, pltpu.roll(own, LANES - 13, 1), pltpu.roll(after, LANES - 13, 1)
            )
            west = jnp.where(lanes >= 13, pltpu.roll(own, 13, 1), pltpu.roll(prior, 13, 1))
            east = jnp.where(ids < count - 16, east, 0.0)
            west = jnp.where(ids >= 16, west, 0.0)
            twin = jnp.where(lanes % 4 == 3, east, jnp.where(lanes % 4 == 0, west, own))
            k = c - t * TILE
            tendency = (third[:, k : k + LANES] + b3_rows).astype(BF).astype(F32)
            value = s_v[:, cols] + TIMESTEP * 0.5 * (own + twin) + tendency
            o_v[:, cols] = jnp.where(ids < count, value, 0.0)
        copy = pltpu.make_async_copy(cut(o_v, t), cut(o_hbm, t), out_sems.at[t])
        copy.start()
        outs.append(copy)
    for copy in outs:
        copy.wait()


def twin_kernel(live_ref, before_ref, after_ref, i_hbm, o_hbm, held, sems):
    del i_hbm
    start = own_live(live_ref) - 16
    block = pl.multiple_of(start // LANES * LANES, LANES)
    spots = [o_hbm.at[:, pl.ds(0, LANES)], o_hbm.at[:, pl.ds(block, LANES)]]
    loads = [pltpu.make_async_copy(spots[k], held.at[k], sems.at[k]) for k in range(2)]
    for copy in loads:
        copy.start()
    pad = jnp.zeros((LANES - 16, LANES), F32)
    half = 0.5 * TIMESTEP
    west = half * jnp.concatenate([before_ref[...], pad], axis=0).T
    east = half * pltpu.roll(jnp.concatenate([after_ref[...], pad], axis=0).T, start - block, 1)
    for copy in loads:
        copy.wait()
    shared = block == 0
    held[0] = held[0] + west + jnp.where(shared, east, 0.0)
    held[1] = held[1] + east + jnp.where(shared, west, 0.0)
    stores = [pltpu.make_async_copy(held.at[k], spots[k], sems.at[k]) for k in range(2)]
    stores[0].start()
    stores[0].wait()
    stores[1].start()
    stores[1].wait()


def passed_along(block, axis, distance):
    devices = range(lax.axis_size(axis))
    route = [((i - distance) % len(devices), i) for i in devices]
    return lax.ppermute(block, axis, route)


def body(state, wind, live, w_first, b_first, w_second, b_second, w_third, b_third):
    fields, levels, columns = state.shape
    features = fields * levels
    units = w_first.shape[1]
    s = state.reshape(features, columns)
    w = wind.reshape(features, columns)
    deriv = deriv_operand()
    smem = pl.BlockSpec(memory_space=pltpu.SMEM)
    vmem = pl.BlockSpec(memory_space=pltpu.VMEM)
    hbm = pl.BlockSpec(memory_space=pltpu.HBM)
    edge = jax.ShapeDtypeStruct((16, LANES), F32)
    last, first = pl.pallas_call(
        edge_kernel,
        out_shape=(edge, edge),
        in_specs=[smem, hbm, hbm, hbm],
        out_specs=(vmem, vmem),
        scratch_shapes=[
            pltpu.VMEM((2, features, LANES), F32),
            pltpu.VMEM((2, features, LANES), F32),
            pltpu.VMEM(deriv.shape, BF),
            pltpu.SemaphoreType.DMA((5,)),
        ],
        compiler_params=pltpu.CompilerParams(vmem_limit_bytes=62 * MIB),
        cost_estimate=pl.CostEstimate(flops=10**7, bytes_accessed=10**5, transcendentals=0),
    )(live, s, w, deriv)
    before = passed_along(last, ("grp", "col"), 1)
    after = passed_along(first, ("grp", "col"), -1)
    operands = [
        s, w, w_first, b_first[None], w_second, b_second[None], w_third, b_third[None], deriv
    ]
    out = pl.pallas_call(
        main_kernel,
        out_shape=jax.ShapeDtypeStruct((features, columns), F32),
        in_specs=[smem] + [hbm] * len(operands),
        out_specs=hbm,
        scratch_shapes=[pltpu.VMEM(a.shape, a.dtype) for a in operands]
        + [
            pltpu.VMEM((LANES, units), BF),
            pltpu.VMEM((columns, units), BF),
            pltpu.VMEM((columns, units), BF),
            pltpu.VMEM((features, columns), F32),
            pltpu.VMEM((features, columns), F32),
            pltpu.SemaphoreType.DMA((12,)),
            pltpu.SemaphoreType.DMA((columns // TILE,)),
        ],
        compiler_params=pltpu.CompilerParams(vmem_limit_bytes=62 * MIB),
        cost_estimate=pl.CostEstimate(
            flops=6 * 10**9, bytes_accessed=6 * 10**6, transcendentals=4 * 10**6
        ),
    )(live, *operands)
    out = pl.pallas_call(
        twin_kernel,
        out_shape=jax.ShapeDtypeStruct((features, columns), F32),
        in_specs=[smem, vmem, vmem, hbm],
        out_specs=hbm,
        scratch_shapes=[pltpu.VMEM((2, features, LANES), F32), pltpu.SemaphoreType.DMA((2,))],
        input_output_aliases={3: 0},
        compiler_params=pltpu.CompilerParams(vmem_limit_bytes=2 * MIB),
    )(live, before, after, out)
    return out.reshape(fields, levels, columns)


def solution(mesh):
    return jax.shard_map(
        body,
        mesh=mesh,
        in_specs=(
            P(None, None, ("grp", "col")),
            P(None, None, ("grp", "col")),
            P("grp", None),
            P(),
            P(),
            P(),
            P(),
            P(),
            P(),
        ),
        out_specs=P(None, None, ("grp", "col")),
        check_vma=False,
    )
```

```python
import functools

import jax
import jax.numpy as jnp
import numpy as np
from jax import lax
from jax.experimental import pallas as pl
from jax.experimental.pallas import tpu as pltpu
from jax.sharding import PartitionSpec as P

TIMESTEP = 0.1
LANES = 128
TILE = 512
CHUNK = 256
BF = jnp.bfloat16
F32 = jnp.float32
MIB = 2**20


def gll_table():
    points = np.array([-1.0, -1.0 / np.sqrt(5.0), 1.0 / np.sqrt(5.0), 1.0])
    legendre = 0.5 * (5.0 * points**3 - 3.0 * points)
    deriv_table = np.zeros((4, 4))
    for i in range(4):
        for j in range(4):
            if i != j:
                deriv_table[i, j] = legendre[i] / (legendre[j] * (points[i] - points[j]))
    deriv_table[0, 0] = -3.0
    deriv_table[3, 3] = 3.0
    return deriv_table


def deriv_operand():
    deriv_table = gll_table()
    along_xi = np.kron(np.eye(8), np.kron(np.eye(4), deriv_table)).T
    along_eta = np.kron(np.eye(8), np.kron(deriv_table, np.eye(4))).T
    both = np.concatenate([along_xi, along_eta], axis=1).astype(np.float32)
    high = both.astype(jnp.bfloat16)
    low = (both - high.astype(np.float32)).astype(jnp.bfloat16)
    return jnp.asarray(np.concatenate([high, high, low], axis=0))


def block_rate(s, wind_xi, wind_eta, deriv):
    high = s.astype(BF)
    low = (s - high.astype(F32)).astype(BF)
    d = jnp.dot(
        jnp.concatenate([high, low, high], axis=1), deriv, preferred_element_type=F32
    )
    return -(wind_xi * d[:, :LANES] + wind_eta * d[:, LANES:])


def both_fields(w):
    return jnp.concatenate([w, w], axis=0)


def lane_ids():
    return lax.broadcasted_iota(jnp.int32, (LANES, LANES), 1)


def own_live(live_ref):
    return live_ref[0, lax.axis_index("col")] * 16


def even_device():
    return lax.axis_index("col") % 2 == 0


def edge_kernel(live_ref, s_hbm, w_hbm, d_hbm, even_ref, odd_ref, s_v, w_v, deriv, sems):
    start = own_live(live_ref) - 16
    block = pl.multiple_of(start // LANES * LANES, LANES)
    copies = [
        pltpu.make_async_copy(s_hbm.at[:, pl.ds(0, LANES)], s_v.at[0], sems.at[0]),
        pltpu.make_async_copy(w_hbm.at[:, pl.ds(0, LANES)], w_v.at[0], sems.at[1]),
        pltpu.make_async_copy(s_hbm.at[:, pl.ds(block, LANES)], s_v.at[1], sems.at[2]),
        pltpu.make_async_copy(w_hbm.at[:, pl.ds(block, LANES)], w_v.at[1], sems.at[3]),
        pltpu.make_async_copy(d_hbm, deriv, sems.at[4]),
    ]
    for copy in copies:
        copy.start()
    for copy in copies:
        copy.wait()
    rates = [
        block_rate(s_v[k], both_fields(w_v[k, 0:64]), both_fields(w_v[k, 64:128]), deriv[...])
        for k in range(2)
    ]
    lanes = lane_ids()
    kept = (lanes < 16) & (lanes % 4 == 0)
    turn = LANES - 3 - (start - block)
    east = pltpu.roll(rates[1], jnp.where(turn < 0, turn + LANES, turn), 1)
    last = jnp.where(kept, east, 0.0)
    first = jnp.where(kept, rates[0], 0.0)
    even = even_device()
    even_ref[...] = jnp.where(even, last, first)
    odd_ref[...] = jnp.where(even, first, last)


def main_kernel(
    live_ref, s_hbm, w_hbm, w1_hbm, b1_hbm, w2_hbm, b2_hbm, w3_hbm, b3_hbm, d_hbm, o_hbm,
    s_v, w_v, w1, b1, w2, b2, w3, b3, deriv, w3t, h1, h2, rate, o_v, in_sems, out_sems,
):
    columns, units = h1.shape
    tiles = columns // TILE
    count = own_live(live_ref)

    def fetch(index, source, target):
        copy = pltpu.make_async_copy(source, target, in_sems.at[index])
        copy.start()
        return copy

    def cut(ref, tile):
        return ref.at[:, pl.ds(tile * TILE, TILE)]

    s_copies = [fetch(0, cut(s_hbm, 0), cut(s_v, 0))]
    early = [fetch(4, w1_hbm, w1), fetch(5, b1_hbm, b1)]
    s_copies += [fetch(t, cut(s_hbm, t), cut(s_v, t)) for t in range(1, tiles)]
    later = [
        fetch(6, w2_hbm, w2),
        fetch(7, b2_hbm, b2),
        fetch(8, w3_hbm, w3),
        fetch(9, b3_hbm, b3),
        fetch(10, d_hbm, deriv),
        fetch(11, w_hbm, w_v),
    ]
    for copy in early:
        copy.wait()
    for t in range(tiles):
        s_copies[t].wait()
        x = s_v[:, t * TILE : (t + 1) * TILE].astype(BF)
        for n in range(0, units, CHUNK):
            a = lax.dot_general(
                x, w1[:, n : n + CHUNK], (((0,), (0,)), ((), ())), preferred_element_type=F32
            )
            h1[t * TILE : (t + 1) * TILE, n : n + CHUNK] = jax.nn.silu(
                a + b1[:, n : n + CHUNK]
            ).astype(BF)
    for copy in later:
        copy.wait()
    w3t[...] = w3[...].T
    b3_rows = jnp.broadcast_to(b3[...], (LANES, LANES)).T
    for c in range(0, columns, LANES):
        cols = slice(c, c + LANES)
        rate[:, cols] = block_rate(
            s_v[:, cols], both_fields(w_v[0:64, cols]), both_fields(w_v[64:128, cols]), deriv[...]
        )
    lanes = lane_ids()
    outs = []
    for t in range(tiles):
        rows = slice(t * TILE, (t + 1) * TILE)
        for n in range(0, units, CHUNK):
            a = jnp.dot(h1[rows], w2[:, n : n + CHUNK], preferred_element_type=F32)
            h2[rows, n : n + CHUNK] = jax.nn.silu(a + b2[:, n : n + CHUNK]).astype(BF)
        third = lax.dot_general(
            w3t[...], h2[rows], (((1,), (1,)), ((), ())), preferred_element_type=F32
        )
        for c in range(t * TILE, (t + 1) * TILE, LANES):
            cols = slice(c, c + LANES)
            own = rate[:, cols]
            after = rate[:, c + LANES : c + 2 * LANES] if c + LANES < columns else own
            prior = rate[:, c - LANES : c] if c else own
            ids = lanes + c
            east = jnp.where(
                lanes < LANES - 13, pltpu.roll(own, LANES - 13, 1), pltpu.roll(after, LANES - 13, 1)
            )
            west = jnp.where(lanes >= 13, pltpu.roll(own, 13, 1), pltpu.roll(prior, 13, 1))
            pair = jnp.where(
                lanes % 4 == 3,
                jnp.where(ids < count - 16, own + east, 0.0),
                jnp.where(lanes % 4 == 0, jnp.where(ids >= 16, own + west, 0.0), own + own),
            )
            k = c - t * TILE
            tendency = (third[:, k : k + LANES] + b3_rows).astype(BF).astype(F32)
            value = s_v[:, cols] + TIMESTEP * 0.5 * pair + tendency
            o_v[:, cols] = jnp.where(ids < count, value, 0.0)
        copy = pltpu.make_async_copy(cut(o_v, t), cut(o_hbm, t), out_sems.at[t])
        copy.start()
        outs.append(copy)
    for copy in outs:
        copy.wait()


def twin_kernel(live_ref, even_hbm, odd_hbm, i_hbm, o_hbm, even_ref, odd_ref, held, sems):
    del i_hbm
    start = own_live(live_ref) - 16
    block = pl.multiple_of(start // LANES * LANES, LANES)
    spots = [o_hbm.at[:, pl.ds(0, LANES)], o_hbm.at[:, pl.ds(block, LANES)]]
    loads = [
        pltpu.make_async_copy(even_hbm, even_ref, sems.at[2]),
        pltpu.make_async_copy(odd_hbm, odd_ref, sems.at[3]),
        pltpu.make_async_copy(spots[0], held.at[0], sems.at[0]),
        pltpu.make_async_copy(spots[1], held.at[1], sems.at[1]),
    ]
    for copy in loads:
        copy.start()
    for copy in loads:
        copy.wait()
    even = even_device()
    half = 0.5 * TIMESTEP
    west = half * jnp.where(even, odd_ref[...], even_ref[...])
    east = half * pltpu.roll(jnp.where(even, even_ref[...], odd_ref[...]), start - block + 3, 1)
    shared = block == 0
    held[0] = held[0] + west + jnp.where(shared, east, 0.0)
    held[1] = held[1] + east + jnp.where(shared, west, 0.0)
    stores = [pltpu.make_async_copy(held.at[k], spots[k], sems.at[k]) for k in range(2)]
    stores[0].start()

    @pl.when(block > 0)
    def _():
        stores[1].start()
        stores[1].wait()

    stores[0].wait()


def pair_sum(block, axis, offset):
    devices = lax.axis_size(axis)
    pairs = [[i, (i + 1) % devices] for i in range(offset, devices, 2)]
    return lax.psum(block, axis, axis_index_groups=pairs)


def body(state, wind, live, w_first, b_first, w_second, b_second, w_third, b_third):
    fields, levels, columns = state.shape
    features = fields * levels
    units = w_first.shape[1]
    s = state.reshape(features, columns)
    w = wind.reshape(features, columns)
    deriv = deriv_operand()
    smem = pl.BlockSpec(memory_space=pltpu.SMEM)
    vmem = pl.BlockSpec(memory_space=pltpu.VMEM)
    hbm = pl.BlockSpec(memory_space=pltpu.HBM)
    edge = jax.ShapeDtypeStruct((features, LANES), F32)
    even, odd = pl.pallas_call(
        edge_kernel,
        out_shape=(edge, edge),
        in_specs=[smem, hbm, hbm, hbm],
        out_specs=(vmem, vmem),
        scratch_shapes=[
            pltpu.VMEM((2, features, LANES), F32),
            pltpu.VMEM((2, features, LANES), F32),
            pltpu.VMEM(deriv.shape, BF),
            pltpu.SemaphoreType.DMA((5,)),
        ],
        compiler_params=pltpu.CompilerParams(vmem_limit_bytes=62 * MIB),
        cost_estimate=pl.CostEstimate(flops=10**7, bytes_accessed=10**5, transcendentals=0),
    )(live, s, w, deriv)
    even = pair_sum(even, ("grp", "col"), 0)
    odd = pair_sum(odd, ("grp", "col"), 1)
    operands = [
        s, w, w_first, b_first[None], w_second, b_second[None], w_third, b_third[None], deriv
    ]
    out = pl.pallas_call(
        main_kernel,
        out_shape=jax.ShapeDtypeStruct((features, columns), F32),
        in_specs=[smem] + [hbm] * len(operands),
        out_specs=hbm,
        scratch_shapes=[pltpu.VMEM(a.shape, a.dtype) for a in operands]
        + [
            pltpu.VMEM((LANES, units), BF),
            pltpu.VMEM((columns, units), BF),
            pltpu.VMEM((columns, units), BF),
            pltpu.VMEM((features, columns), F32),
            pltpu.VMEM((features, columns), F32),
            pltpu.SemaphoreType.DMA((12,)),
            pltpu.SemaphoreType.DMA((columns // TILE,)),
        ],
        compiler_params=pltpu.CompilerParams(vmem_limit_bytes=62 * MIB),
        cost_estimate=pl.CostEstimate(
            flops=6 * 10**9, bytes_accessed=6 * 10**6, transcendentals=4 * 10**6
        ),
    )(live, *operands)
    out = pl.pallas_call(
        twin_kernel,
        out_shape=jax.ShapeDtypeStruct((features, columns), F32),
        in_specs=[smem, hbm, hbm, hbm],
        out_specs=hbm,
        scratch_shapes=[
            pltpu.VMEM(even.shape, F32),
            pltpu.VMEM(odd.shape, F32),
            pltpu.VMEM((2, features, LANES), F32),
            pltpu.SemaphoreType.DMA((4,)),
        ],
        input_output_aliases={3: 0},
        compiler_params=pltpu.CompilerParams(vmem_limit_bytes=62 * MIB),
    )(live, even, odd, out)
    return out.reshape(fields, levels, columns)


def solution(mesh):
    return jax.shard_map(
        body,
        mesh=mesh,
        in_specs=(
            P(None, None, ("grp", "col")),
            P(None, None, ("grp", "col")),
            P("grp", None),
            P(),
            P(),
            P(),
            P(),
            P(),
            P(),
        ),
        out_specs=P(None, None, ("grp", "col")),
        check_vma=False,
    )
```

```python
import functools

import jax
import jax.numpy as jnp
import numpy as np
from jax import lax
from jax.experimental import pallas as pl
from jax.experimental.pallas import tpu as pltpu
from jax.sharding import PartitionSpec as P

TIMESTEP = 0.1
LANES = 128
TILE = 512
EARLY = ((3, 2, 2, 1, 1, 0, 0, 0), (2, 1, 1, 0, 0, 0, 0, 0))
CHUNK = 256
BF = jnp.bfloat16
F32 = jnp.float32
MIB = 2**20


def gll_table():
    points = np.array([-1.0, -1.0 / np.sqrt(5.0), 1.0 / np.sqrt(5.0), 1.0])
    legendre = 0.5 * (5.0 * points**3 - 3.0 * points)
    deriv_table = np.zeros((4, 4))
    for i in range(4):
        for j in range(4):
            if i != j:
                deriv_table[i, j] = legendre[i] / (legendre[j] * (points[i] - points[j]))
    deriv_table[0, 0] = -3.0
    deriv_table[3, 3] = 3.0
    return deriv_table


def deriv_operand():
    deriv_table = gll_table()
    along_xi = np.kron(np.eye(8), np.kron(np.eye(4), deriv_table)).T
    along_eta = np.kron(np.eye(8), np.kron(deriv_table, np.eye(4))).T
    both = np.concatenate([along_xi, along_eta], axis=1).astype(np.float32)
    high = both.astype(jnp.bfloat16)
    low = (both - high.astype(np.float32)).astype(jnp.bfloat16)
    return jnp.asarray(np.concatenate([high, high, low], axis=0))


def block_rate(s, wind_xi, wind_eta, deriv):
    high = s.astype(BF)
    low = (s - high.astype(F32)).astype(BF)
    d = jnp.dot(
        jnp.concatenate([high, low, high], axis=1), deriv, preferred_element_type=F32
    )
    return -(wind_xi * d[:, :LANES] + wind_eta * d[:, LANES:])


def both_fields(w):
    return jnp.concatenate([w, w], axis=0)


def lane_ids():
    return lax.broadcasted_iota(jnp.int32, (LANES, LANES), 1)


def own_live(live_ref):
    return live_ref[0, lax.axis_index("col")] * 16


def early_tiles():
    col = lax.axis_index("col")
    amount = 0
    for z in range(8):
        here = jnp.where(col // 8 == 0, EARLY[0][z], EARLY[1][z])
        amount = jnp.where(col % 8 == z, here, amount)
    return amount


def fetch(source, target, sems, index):
    copy = pltpu.make_async_copy(source, target, sems.at[index])
    copy.start()
    return copy


def edge_fetches(live_ref, s_hbm, w_hbm, d_hbm, deriv, s_v, w_v, sems):
    start = own_live(live_ref) - 16
    block = pl.multiple_of(start // LANES * LANES, LANES)
    return [
        fetch(s_hbm.at[:, pl.ds(0, LANES)], s_v.at[0], sems, 0),
        fetch(w_hbm.at[:, pl.ds(0, LANES)], w_v.at[0], sems, 1),
        fetch(s_hbm.at[:, pl.ds(block, LANES)], s_v.at[1], sems, 2),
        fetch(w_hbm.at[:, pl.ds(block, LANES)], w_v.at[1], sems, 3),
        fetch(d_hbm, deriv, sems, 4),
    ]


def edge_rates(copies, live_ref, deriv, s_v, w_v):
    start = own_live(live_ref) - 16
    block = start // LANES * LANES
    for copy in copies:
        copy.wait()
    turn = jnp.where(start > block, LANES - (start - block), 0)
    lanes = lane_ids()

    def joined(first, last):
        return jnp.where(lanes < 16, first, pltpu.roll(last, lax.rem(turn + 16, LANES), 1))

    s = joined(s_v[0], s_v[1])
    w = joined(w_v[0], w_v[1])
    rate = block_rate(s, both_fields(w[0:64]), both_fields(w[64:128]), deriv[...])
    turned = rate.T
    rows = lax.broadcasted_iota(jnp.int32, (16, LANES), 0)
    east = pltpu.roll(turned[16:32], 13, 0)
    west = pltpu.roll(turned[0:16], 3, 0)
    return jnp.where(rows % 4 == 0, east, 0.0), jnp.where(rows % 4 == 3, west, 0.0)


def network_parts(hbm, vmem, sems, first_sem):
    return [fetch(a, b, sems, first_sem + k) for k, (a, b) in enumerate(zip(hbm, vmem))]


def columns_at(tile, size=TILE):
    return pl.ds(pl.multiple_of(tile * size, size), size)


def first_layer(tile, s_v, w1, b1, h1, size=TILE):
    units = h1.shape[1]
    x = s_v[:, columns_at(tile, size)].astype(BF)
    for n in range(0, units, CHUNK):
        a = lax.dot_general(
            x, w1[:, n : n + CHUNK], (((0,), (0,)), ((), ())), preferred_element_type=F32
        )
        h1[columns_at(tile, size), n : n + CHUNK] = jax.nn.silu(a + b1[:, n : n + CHUNK]).astype(BF)


def rate_at(block, s_v, w_v, deriv, rate, slot):
    cols = pl.ds(pl.multiple_of(block * LANES, LANES), LANES)
    rate[:, pl.ds(pl.multiple_of(slot * LANES + LANES, LANES), LANES)] = block_rate(
        s_v[:, cols], both_fields(w_v[0:64, cols]), both_fields(w_v[64:128, cols]), deriv[...]
    )


def finish_tile(tile, count, s_v, w2, b2, w3t, b3_rows, h1, h2, rate, o_v, size=TILE):
    units = h1.shape[1]
    h = h1[columns_at(tile, size), :]
    for n in range(0, units, CHUNK):
        a = jnp.dot(h, w2[:, n : n + CHUNK], preferred_element_type=F32)
        h2[0:size, n : n + CHUNK] = jax.nn.silu(a + b2[:, n : n + CHUNK]).astype(BF)
    third = lax.dot_general(
        w3t[...], h2[0:size], (((1,), (1,)), ((), ())), preferred_element_type=F32
    )
    lanes = lane_ids()
    for k in range(0, size, LANES):
        base = pl.multiple_of(tile * size + k, LANES)
        own = rate[:, pl.ds(base + LANES, LANES)]
        after = rate[:, pl.ds(base + 2 * LANES, LANES)]
        prior = rate[:, pl.ds(base, LANES)]
        ids = lanes + base
        east = pltpu.roll(jnp.where(lanes < 13, after, own), LANES - 13, 1)
        west = pltpu.roll(jnp.where(lanes >= LANES - 13, prior, own), 13, 1)
        east = jnp.where(ids < count - 16, east, 0.0)
        west = jnp.where(ids >= 16, west, 0.0)
        twin = jnp.where(lanes % 4 == 3, east, jnp.where(lanes % 4 == 0, west, own))
        tendency = (third[:, k : k + LANES] + b3_rows[...]).astype(BF).astype(F32)
        value = s_v[:, pl.ds(base, LANES)] + (0.5 * TIMESTEP) * (own + twin) + tendency
        o_v[:, pl.ds(base, LANES)] = jnp.where(ids < count, value, 0.0)


def ready_last(w3, b3, w3t, b3_rows):
    w3t[...] = w3[...].T
    b3_rows[...] = jnp.broadcast_to(b3[...], (LANES, LANES)).T


def do_tiles(tiles, count, begun, refs, o_hbm, sem):
    s_v, w1, b1, w2, b2, w3, b3, deriv, w_v, w3t, b3_rows, h1, h2, rate, o_v = refs
    for copy in begun[:3]:
        copy.wait()
    for tile in tiles:
        first_layer(tile, s_v, w1, b1, h1)
    for copy in begun[3:]:
        copy.wait()
    ready_last(w3, b3, w3t, b3_rows)
    per = TILE // LANES
    for block in range(max(tiles[0] * per - 1, 0), min(tiles[-1] * per + per + 1, s_v.shape[1] // LANES)):
        rate_at(block, s_v, w_v, deriv, rate, block)

    def out_copy(tile):
        cols = columns_at(tile)
        return pltpu.make_async_copy(o_v.at[:, cols], o_hbm.at[:, cols], sem)

    for tile in tiles:
        finish_tile(tile, count, s_v, w2, b2, w3t, b3_rows, h1, h2, rate, o_v)
        out_copy(tile).start()
    for tile in tiles:
        out_copy(tile).wait()


def edge_kernel(live_ref, s_hbm, w_hbm, d_hbm, last_ref, first_ref, s_e, w_e, deriv, sems):
    copies = edge_fetches(live_ref, s_hbm, w_hbm, d_hbm, deriv, s_e, w_e, sems)
    last_ref[...], first_ref[...] = edge_rates(copies, live_ref, deriv, s_e, w_e)


def early_kernel(
    live_ref, first_ref, s_v, w_v, w1, b1, w2, b2, w3, b3, deriv, passed_ref, o_hbm,
    w3t, b3_rows, h1, h2, rate, o_v, sems,
):
    early = early_tiles()
    refs = [s_v, w1, b1, w2, b2, w3, b3, deriv, w_v, w3t, b3_rows, h1, h2, rate, o_v]
    for amount in sorted(set(EARLY[0] + EARLY[1]) - {0}):

        @pl.when(early == amount)
        def _():
            do_tiles(range(amount), own_live(live_ref), [], refs, o_hbm, sems.at[0])

    passed_ref[...] = first_ref[...]


def late_kernel(
    live_ref, s_v, w_v, w1, b1, w2, b2, w3, b3, deriv, i_hbm, o_hbm,
    w3t, b3_rows, h1, h2, rate, o_v, sems,
):
    del i_hbm
    early = early_tiles()
    refs = [s_v, w1, b1, w2, b2, w3, b3, deriv, w_v, w3t, b3_rows, h1, h2, rate, o_v]
    tiles = s_v.shape[1] // TILE
    for amount in sorted(set(EARLY[0] + EARLY[1]) | {0}):

        @pl.when(early == amount)
        def _():
            do_tiles(range(amount, tiles), own_live(live_ref), [], refs, o_hbm, sems.at[0])


def twin_kernel(live_ref, after_ref, before_ref, i_hbm, o_hbm, held, sems):
    del i_hbm
    start = own_live(live_ref) - 16
    block = pl.multiple_of(start // LANES * LANES, LANES)
    spots = [o_hbm.at[:, pl.ds(0, LANES)], o_hbm.at[:, pl.ds(block, LANES)]]
    loads = [pltpu.make_async_copy(spots[k], held.at[k], sems.at[k]) for k in range(2)]
    for copy in loads:
        copy.start()
    pad = jnp.zeros((LANES - 16, LANES), F32)
    half = 0.5 * TIMESTEP
    west = half * jnp.concatenate([before_ref[...], pad], axis=0).T
    east = half * pltpu.roll(jnp.concatenate([after_ref[...], pad], axis=0).T, start - block, 1)
    for copy in loads:
        copy.wait()
    shared = block == 0
    held[0] = held[0] + west + jnp.where(shared, east, 0.0)
    held[1] = held[1] + east + jnp.where(shared, west, 0.0)
    stores = [pltpu.make_async_copy(held.at[k], spots[k], sems.at[k]) for k in range(2)]
    stores[0].start()

    @pl.when(block > 0)
    def _():
        stores[1].start()
        stores[1].wait()

    stores[0].wait()


def passed_along(block, axis, distance):
    devices = range(lax.axis_size(axis))
    route = [((i - distance) % len(devices), i) for i in devices]
    return lax.ppermute(block, axis, route)


def body(state, wind, live, w_first, b_first, w_second, b_second, w_third, b_third):
    fields, levels, columns = state.shape
    features = fields * levels
    units = w_first.shape[1]
    s = state.reshape(features, columns)
    w = wind.reshape(features, columns)
    deriv = deriv_operand()
    smem = pl.BlockSpec(memory_space=pltpu.SMEM)
    vmem = pl.BlockSpec(memory_space=pltpu.VMEM)
    hbm = pl.BlockSpec(memory_space=pltpu.HBM)
    edge = jax.ShapeDtypeStruct((16, LANES), F32)
    whole = jax.ShapeDtypeStruct((features, columns), F32)
    operands = [
        s, w, w_first, b_first[None], w_second, b_second[None], w_third, b_third[None], deriv
    ]
    work = [
        pltpu.VMEM((LANES, units), BF),
        pltpu.VMEM((LANES, LANES), F32),
        pltpu.VMEM((columns, units), BF),
        pltpu.VMEM((TILE, units), BF),
        pltpu.VMEM((features, columns + 2 * LANES), F32),
        pltpu.VMEM((features, columns), F32),
    ]
    pair = pltpu.VMEM((2, features, LANES), F32)
    last, first = pl.pallas_call(
        edge_kernel,
        out_shape=(edge, edge),
        in_specs=[smem, hbm, hbm, hbm],
        out_specs=(vmem, vmem),
        scratch_shapes=[pair, pair, pltpu.VMEM(deriv.shape, BF), pltpu.SemaphoreType.DMA((5,))],
        compiler_params=pltpu.CompilerParams(vmem_limit_bytes=54 * MIB),
        cost_estimate=pl.CostEstimate(flops=4 * 10**9, bytes_accessed=10**5, transcendentals=0),
    )(live, s, w, deriv)
    before = passed_along(last, ("grp", "col"), 1)
    work.append(pltpu.SemaphoreType.DMA((1,)))
    params = pltpu.CompilerParams(vmem_limit_bytes=28 * MIB)
    first, out = pl.pallas_call(
        early_kernel,
        out_shape=(edge, whole),
        in_specs=[smem, vmem] + [vmem] * len(operands),
        out_specs=(vmem, hbm),
        scratch_shapes=work,
        compiler_params=params,
    )(live, first, *operands)
    after = passed_along(first, ("grp", "col"), -1)
    out = pl.pallas_call(
        late_kernel,
        out_shape=whole,
        in_specs=[smem] + [vmem] * len(operands) + [hbm],
        out_specs=hbm,
        scratch_shapes=work,
        input_output_aliases={1 + len(operands): 0},
        compiler_params=params,
        cost_estimate=pl.CostEstimate(
            flops=6 * 10**9, bytes_accessed=6 * 10**6, transcendentals=4 * 10**6
        ),
    )(live, *operands, out)
    out = pl.pallas_call(
        twin_kernel,
        out_shape=whole,
        in_specs=[smem, vmem, vmem, hbm],
        out_specs=hbm,
        scratch_shapes=[pair, pltpu.SemaphoreType.DMA((2,))],
        input_output_aliases={3: 0},
        compiler_params=pltpu.CompilerParams(vmem_limit_bytes=2 * MIB),
    )(live, after, before, out)
    return out.reshape(fields, levels, columns)


def solution(mesh):
    return jax.shard_map(
        body,
        mesh=mesh,
        in_specs=(
            P(None, None, ("grp", "col")),
            P(None, None, ("grp", "col")),
            P("grp", None),
            P(),
            P(),
            P(),
            P(),
            P(),
            P(),
        ),
        out_specs=P(None, None, ("grp", "col")),
        check_vma=False,
    )
```

```python
import functools

import jax
import jax.numpy as jnp
import numpy as np
from jax import lax
from jax.experimental import pallas as pl
from jax.experimental.pallas import tpu as pltpu
from jax.sharding import PartitionSpec as P

TIMESTEP = 0.1
LANES = 128
TILE = 512
HALF = 256
EARLY = ((6, 6, 4, 2, 2, 1, 1, 0), (2, 2, 2, 1, 1, 0, 0, 0))
CHUNK = 256
BF = jnp.bfloat16
F32 = jnp.float32
MIB = 2**20


def gll_table():
    points = np.array([-1.0, -1.0 / np.sqrt(5.0), 1.0 / np.sqrt(5.0), 1.0])
    legendre = 0.5 * (5.0 * points**3 - 3.0 * points)
    deriv_table = np.zeros((4, 4))
    for i in range(4):
        for j in range(4):
            if i != j:
                deriv_table[i, j] = legendre[i] / (legendre[j] * (points[i] - points[j]))
    deriv_table[0, 0] = -3.0
    deriv_table[3, 3] = 3.0
    return deriv_table


def deriv_operand():
    deriv_table = gll_table()
    along_xi = np.kron(np.eye(8), np.kron(np.eye(4), deriv_table)).T
    along_eta = np.kron(np.eye(8), np.kron(deriv_table, np.eye(4))).T
    both = np.concatenate([along_xi, along_eta], axis=1).astype(np.float32)
    high = both.astype(jnp.bfloat16)
    low = (both - high.astype(np.float32)).astype(jnp.bfloat16)
    return jnp.asarray(np.concatenate([high, high, low], axis=0))


def block_rate(s, wind_xi, wind_eta, deriv):
    high = s.astype(BF)
    low = (s - high.astype(F32)).astype(BF)
    d = jnp.dot(
        jnp.concatenate([high, low, high], axis=1), deriv, preferred_element_type=F32
    )
    return -(wind_xi * d[:, :LANES] + wind_eta * d[:, LANES:])


def both_fields(w):
    return jnp.concatenate([w, w], axis=0)


def lane_ids():
    return lax.broadcasted_iota(jnp.int32, (LANES, LANES), 1)


def own_live(live_ref):
    return live_ref[0, lax.axis_index("col")] * 16


def early_tiles():
    col = lax.axis_index("col")
    amount = 0
    for z in range(8):
        here = jnp.where(col // 8 == 0, EARLY[0][z], EARLY[1][z])
        amount = jnp.where(col % 8 == z, here, amount)
    return amount


def fetch(source, target, sems, index):
    copy = pltpu.make_async_copy(source, target, sems.at[index])
    copy.start()
    return copy


def last_block(count):
    return pl.multiple_of((count - 16) // LANES * LANES, LANES)


def edge_of(rate, lanes_back, row):
    turn = jnp.where(lanes_back > 0, LANES - lanes_back, 0)
    turned = pltpu.roll(rate, turn, 1).T[0:16]
    rows = lax.broadcasted_iota(jnp.int32, (16, LANES), 0)
    return jnp.where(rows % 4 == row, turned, 0.0)


def first_layer(at, s_v, w1, b1, h1, size):
    units = h1.shape[1]
    x = s_v[:, at : at + size].astype(BF)
    for n in range(0, units, CHUNK):
        a = lax.dot_general(
            x, w1[:, n : n + CHUNK], (((0,), (0,)), ((), ())), preferred_element_type=F32
        )
        h1[at : at + size, n : n + CHUNK] = jax.nn.silu(a + b1[:, n : n + CHUNK]).astype(BF)


def rate_at(block, s_v, w_v, deriv, rate, slot):
    cols = pl.ds(pl.multiple_of(block * LANES, LANES), LANES)
    rate[:, pl.ds(pl.multiple_of(slot * LANES + LANES, LANES), LANES)] = block_rate(
        s_v[:, cols], both_fields(w_v[0:64, cols]), both_fields(w_v[64:128, cols]), deriv[...]
    )


def finish_tile(at, count, s_v, w2, b2, w3t, b3_rows, h1, h2, rate, o_v, size):
    units = h1.shape[1]
    h = h1[at : at + size, :]
    for n in range(0, units, CHUNK):
        a = jnp.dot(h, w2[:, n : n + CHUNK], preferred_element_type=F32)
        h2[0:size, n : n + CHUNK] = jax.nn.silu(a + b2[:, n : n + CHUNK]).astype(BF)
    third = lax.dot_general(
        w3t[...], h2[0:size], (((1,), (1,)), ((), ())), preferred_element_type=F32
    )
    lanes = lane_ids()
    for k in range(0, size, LANES):
        base = at + k
        own = rate[:, pl.ds(base + LANES, LANES)]
        after = rate[:, pl.ds(base + 2 * LANES, LANES)]
        prior = rate[:, pl.ds(base, LANES)]
        ids = lanes + base
        east = pltpu.roll(jnp.where(lanes < 13, after, own), LANES - 13, 1)
        west = pltpu.roll(jnp.where(lanes >= LANES - 13, prior, own), 13, 1)
        east = jnp.where(ids < count - 16, east, 0.0)
        west = jnp.where(ids >= 16, west, 0.0)
        twin = jnp.where(lanes % 4 == 3, east, jnp.where(lanes % 4 == 0, west, own))
        tendency = (third[:, k : k + LANES] + b3_rows[...]).astype(BF).astype(F32)
        value = s_v[:, pl.ds(base, LANES)] + (0.5 * TIMESTEP) * (own + twin) + tendency
        o_v[:, pl.ds(base, LANES)] = jnp.where(ids < count, value, 0.0)


def ready_last(w3, b3, w3t, b3_rows):
    w3t[...] = w3[...].T
    b3_rows[...] = jnp.broadcast_to(b3[...], (LANES, LANES)).T


def do_tiles(begin, end, count, refs, held_ref, o_hbm, sem):
    s_v, w1, b1, w2, b2, w3, b3, deriv, w_v, w3t, b3_rows, h1, h2, rate, o_v = refs
    spans = [(begin, 1)] if (end - begin) % 2 else []
    spans += [(at, 2) for at in range(begin + len(spans), end, 2)]
    spans = [(at * HALF, size * HALF) for at, size in spans]
    for at, size in spans:
        first_layer(at, s_v, w1, b1, h1, size)
    ready_last(w3, b3, w3t, b3_rows)
    blocks = s_v.shape[1] // LANES
    per = HALF // LANES
    for block in range(max(begin * per - 1, 0), min(end * per + 1, blocks)):
        rate_at(block, s_v, w_v, deriv, rate, block)
    copies = []
    for at, size in spans:
        finish_tile(at, count, s_v, w2, b2, w3t, b3_rows, h1, h2, rate, o_v, size)
        cols = pl.ds(at, size)
        copies.append(pltpu.make_async_copy(o_v.at[:, cols], o_hbm.at[:, cols], sem))
        copies[-1].start()
    if begin == 0:
        held_ref[0] = o_v[:, 0:LANES]
    held_ref[1] = o_v[:, pl.ds(last_block(count), LANES)]
    for copy in copies:
        copy.wait()


def edge_kernel(live_ref, s_hbm, w_hbm, d_hbm, last_ref, s_e, w_e, deriv, sems):
    start = own_live(live_ref) - 16
    block = pl.multiple_of(start // LANES * LANES, LANES)
    copies = [
        fetch(s_hbm.at[:, pl.ds(block, LANES)], s_e, sems, 0),
        fetch(w_hbm.at[:, pl.ds(block, LANES)], w_e, sems, 1),
        fetch(d_hbm, deriv, sems, 2),
    ]
    for copy in copies:
        copy.wait()
    rate = block_rate(s_e[...], both_fields(w_e[0:64]), both_fields(w_e[64:128]), deriv[...])
    last_ref[...] = edge_of(rate, start - block + 3, 0)


def early_kernel(
    live_ref, last_ref, s_v, w_v, w1, b1, w2, b2, w3, b3, deriv, first_ref, held_ref, o_hbm,
    w3t, b3_rows, h1, h2, rate, o_v, sems,
):
    del last_ref
    rate_at(0, s_v, w_v, deriv, rate, 0)
    first_ref[...] = edge_of(rate[:, LANES : 2 * LANES], LANES - 3, 3)
    early = early_tiles()
    refs = [s_v, w1, b1, w2, b2, w3, b3, deriv, w_v, w3t, b3_rows, h1, h2, rate, o_v]
    for amount in sorted(set(EARLY[0] + EARLY[1]) - {0}):

        @pl.when(early == amount)
        def _():
            do_tiles(0, amount, own_live(live_ref), refs, held_ref, o_hbm, sems.at[0])


def late_kernel(
    live_ref, s_v, w_v, w1, b1, w2, b2, w3, b3, deriv, i_hbm, held_ref, o_hbm,
    w3t, b3_rows, h1, h2, rate, o_v, sems,
):
    del i_hbm
    early = early_tiles()
    refs = [s_v, w1, b1, w2, b2, w3, b3, deriv, w_v, w3t, b3_rows, h1, h2, rate, o_v]
    tiles = s_v.shape[1] // HALF
    for amount in sorted(set(EARLY[0] + EARLY[1]) | {0}):

        @pl.when(early == amount)
        def _():
            do_tiles(amount, tiles, own_live(live_ref), refs, held_ref, o_hbm, sems.at[0])


def twin_kernel(
    live_ref, after_ref, before_ref, early_ref, late_ref, i_hbm, o_hbm, held, sems
):
    del i_hbm
    count = own_live(live_ref)
    block = last_block(count)
    border = early_tiles() * HALF
    pad = jnp.zeros((LANES - 16, LANES), F32)
    half = 0.5 * TIMESTEP
    west = half * jnp.concatenate([before_ref[...], pad], axis=0).T
    east = half * pltpu.roll(
        jnp.concatenate([after_ref[...], pad], axis=0).T, count - 16 - block, 1
    )
    shared = block == 0
    begun = jnp.where(border > 0, early_ref[0], late_ref[0])
    ended = jnp.where(block < border, early_ref[1], late_ref[1])
    held[0] = begun + west + jnp.where(shared, east, 0.0)
    held[1] = ended + east
    stores = [
        pltpu.make_async_copy(held.at[0], o_hbm.at[:, pl.ds(0, LANES)], sems.at[0]),
        pltpu.make_async_copy(held.at[1], o_hbm.at[:, pl.ds(block, LANES)], sems.at[1]),
    ]
    stores[0].start()

    @pl.when(block > 0)
    def _():
        stores[1].start()
        stores[1].wait()

    stores[0].wait()


def passed_along(block, axis, distance):
    devices = range(lax.axis_size(axis))
    route = [((i - distance) % len(devices), i) for i in devices]
    return lax.ppermute(block, axis, route)


def body(state, wind, live, w_first, b_first, w_second, b_second, w_third, b_third):
    fields, levels, columns = state.shape
    features = fields * levels
    units = w_first.shape[1]
    s = state.reshape(features, columns)
    w = wind.reshape(features, columns)
    deriv = deriv_operand()
    smem = pl.BlockSpec(memory_space=pltpu.SMEM)
    vmem = pl.BlockSpec(memory_space=pltpu.VMEM)
    hbm = pl.BlockSpec(memory_space=pltpu.HBM)
    edge = jax.ShapeDtypeStruct((16, LANES), F32)
    whole = jax.ShapeDtypeStruct((features, columns), F32)
    operands = [
        s, w, w_first, b_first[None], w_second, b_second[None], w_third, b_third[None], deriv
    ]
    work = [
        pltpu.VMEM((LANES, units), BF),
        pltpu.VMEM((LANES, LANES), F32),
        pltpu.VMEM((columns, units), BF),
        pltpu.VMEM((TILE, units), BF),
        pltpu.VMEM((features, columns + 2 * LANES), F32),
        pltpu.VMEM((features, columns), F32),
    ]
    pair = pltpu.VMEM((2, features, LANES), F32)
    pair_out = jax.ShapeDtypeStruct((2, features, LANES), F32)
    block = pltpu.VMEM((features, LANES), F32)
    last = pl.pallas_call(
        edge_kernel,
        out_shape=edge,
        in_specs=[smem, hbm, hbm, hbm],
        out_specs=vmem,
        scratch_shapes=[block, block, pltpu.VMEM(deriv.shape, BF), pltpu.SemaphoreType.DMA((3,))],
        compiler_params=pltpu.CompilerParams(vmem_limit_bytes=54 * MIB - 128 * 1024),
        cost_estimate=pl.CostEstimate(flops=4 * 10**9, bytes_accessed=10**5, transcendentals=0),
    )(live, s, w, deriv)
    before = passed_along(last, ("grp", "col"), 1)
    work.append(pltpu.SemaphoreType.DMA((1,)))
    params = pltpu.CompilerParams(vmem_limit_bytes=28 * MIB)
    first, held, out = pl.pallas_call(
        early_kernel,
        out_shape=(edge, pair_out, whole),
        in_specs=[smem, vmem] + [vmem] * len(operands),
        out_specs=(vmem, vmem, hbm),
        scratch_shapes=work,
        compiler_params=params,
    )(live, last, *operands)
    after = passed_along(first, ("grp", "col"), -1)
    rest, out = pl.pallas_call(
        late_kernel,
        out_shape=(pair_out, whole),
        in_specs=[smem] + [vmem] * len(operands) + [hbm],
        out_specs=(vmem, hbm),
        scratch_shapes=work,
        input_output_aliases={1 + len(operands): 1},
        compiler_params=params,
        cost_estimate=pl.CostEstimate(
            flops=6 * 10**9, bytes_accessed=6 * 10**6, transcendentals=4 * 10**6
        ),
    )(live, *operands, out)
    out = pl.pallas_call(
        twin_kernel,
        out_shape=whole,
        in_specs=[smem] + [vmem] * 4 + [hbm],
        out_specs=hbm,
        scratch_shapes=[pair, pltpu.SemaphoreType.DMA((2,))],
        input_output_aliases={5: 0},
        compiler_params=pltpu.CompilerParams(vmem_limit_bytes=2 * MIB),
    )(live, after, before, held, rest, out)
    return out.reshape(fields, levels, columns)


def solution(mesh):
    return jax.shard_map(
        body,
        mesh=mesh,
        in_specs=(
            P(None, None, ("grp", "col")),
            P(None, None, ("grp", "col")),
            P("grp", None),
            P(),
            P(),
            P(),
            P(),
            P(),
            P(),
        ),
        out_specs=P(None, None, ("grp", "col")),
        check_vma=False,
    )
```

```python
import functools

import jax
import jax.numpy as jnp
import numpy as np
from jax import lax
from jax.experimental import pallas as pl
from jax.experimental.pallas import tpu as pltpu
from jax.sharding import PartitionSpec as P

TIMESTEP = 0.1
LANES = 128
TILE = 512
HALF = 256
EARLY = ((6, 6, 6, 4, 4, 2, 1, 0), (2, 2, 2, 1, 1, 0, 0, 0))
CHUNK = 256
BF = jnp.bfloat16
F32 = jnp.float32
MIB = 2**20


def gll_table():
    points = np.array([-1.0, -1.0 / np.sqrt(5.0), 1.0 / np.sqrt(5.0), 1.0])
    legendre = 0.5 * (5.0 * points**3 - 3.0 * points)
    deriv_table = np.zeros((4, 4))
    for i in range(4):
        for j in range(4):
            if i != j:
                deriv_table[i, j] = legendre[i] / (legendre[j] * (points[i] - points[j]))
    deriv_table[0, 0] = -3.0
    deriv_table[3, 3] = 3.0
    return deriv_table


def deriv_operand():
    deriv_table = gll_table()
    along_xi = np.kron(np.eye(8), np.kron(np.eye(4), deriv_table)).T
    along_eta = np.kron(np.eye(8), np.kron(deriv_table, np.eye(4))).T
    both = np.concatenate([along_xi, along_eta], axis=1).astype(np.float32)
    high = both.astype(jnp.bfloat16)
    low = (both - high.astype(np.float32)).astype(jnp.bfloat16)
    return jnp.asarray(np.concatenate([high, high, low], axis=0))


def block_rate(s, wind_xi, wind_eta, deriv):
    high = s.astype(BF)
    low = (s - high.astype(F32)).astype(BF)
    d = jnp.dot(
        jnp.concatenate([high, low, high], axis=1), deriv, preferred_element_type=F32
    )
    return -(wind_xi * d[:, :LANES] + wind_eta * d[:, LANES:])


def both_fields(w):
    return jnp.concatenate([w, w], axis=0)


def lane_ids():
    return lax.broadcasted_iota(jnp.int32, (LANES, LANES), 1)


def own_live(live_ref):
    return live_ref[0, lax.axis_index("col")] * 16


def early_tiles():
    col = lax.axis_index("col")
    amount = 0
    for z in range(8):
        here = jnp.where(col // 8 == 0, EARLY[0][z], EARLY[1][z])
        amount = jnp.where(col % 8 == z, here, amount)
    return amount


def fetch(source, target, sems, index):
    copy = pltpu.make_async_copy(source, target, sems.at[index])
    copy.start()
    return copy


def last_block(count):
    return pl.multiple_of((count - 16) // LANES * LANES, LANES)


def edge_of(rate, lanes_back, row):
    turn = jnp.where(lanes_back > 0, LANES - lanes_back, 0)
    turned = pltpu.roll(rate, turn, 1).T[0:16]
    rows = lax.broadcasted_iota(jnp.int32, (16, LANES), 0)
    return jnp.where(rows % 4 == row, turned, 0.0)


def first_layer(at, s_v, w1, b1, h1, size):
    units = h1.shape[1]
    x = s_v[:, at : at + size].astype(BF)
    for n in range(0, units, CHUNK):
        a = lax.dot_general(
            x, w1[:, n : n + CHUNK], (((0,), (0,)), ((), ())), preferred_element_type=F32
        )
        h1[at : at + size, n : n + CHUNK] = jax.nn.silu(a + b1[:, n : n + CHUNK]).astype(BF)


def rate_at(block, s_v, w_v, deriv, rate, slot):
    cols = pl.ds(pl.multiple_of(block * LANES, LANES), LANES)
    rate[:, pl.ds(pl.multiple_of(slot * LANES + LANES, LANES), LANES)] = block_rate(
        s_v[:, cols], both_fields(w_v[0:64, cols]), both_fields(w_v[64:128, cols]), deriv[...]
    )


def finish_tile(at, count, s_v, w2, b2, w3t, b3_rows, h1, h2, rate, o_v, size):
    units = h1.shape[1]
    h = h1[at : at + size, :]
    for n in range(0, units, CHUNK):
        a = jnp.dot(h, w2[:, n : n + CHUNK], preferred_element_type=F32)
        h2[0:size, n : n + CHUNK] = jax.nn.silu(a + b2[:, n : n + CHUNK]).astype(BF)
    third = lax.dot_general(
        w3t[...], h2[0:size], (((1,), (1,)), ((), ())), preferred_element_type=F32
    )
    lanes = lane_ids()
    for k in range(0, size, LANES):
        base = at + k
        own = rate[:, pl.ds(base + LANES, LANES)]
        after = rate[:, pl.ds(base + 2 * LANES, LANES)]
        prior = rate[:, pl.ds(base, LANES)]
        ids = lanes + base
        east = pltpu.roll(jnp.where(lanes < 13, after, own), LANES - 13, 1)
        west = pltpu.roll(jnp.where(lanes >= LANES - 13, prior, own), 13, 1)
        east = jnp.where(ids < count - 16, east, 0.0)
        west = jnp.where(ids >= 16, west, 0.0)
        twin = jnp.where(lanes % 4 == 3, east, jnp.where(lanes % 4 == 0, west, own))
        tendency = (third[:, k : k + LANES] + b3_rows[...]).astype(BF).astype(F32)
        value = s_v[:, pl.ds(base, LANES)] + (0.5 * TIMESTEP) * (own + twin) + tendency
        o_v[:, pl.ds(base, LANES)] = jnp.where(ids < count, value, 0.0)


def ready_last(w3, b3, w3t, b3_rows):
    w3t[...] = w3[...].T
    b3_rows[...] = jnp.broadcast_to(b3[...], (LANES, LANES)).T


def do_tiles(begin, end, count, refs, held_ref, o_hbm, sem):
    s_v, w1, b1, w2, b2, w3, b3, deriv, w_v, w3t, b3_rows, h1, h2, rate, o_v = refs
    spans = [(begin, 1)] if (end - begin) % 2 else []
    spans += [(at, 2) for at in range(begin + len(spans), end, 2)]
    spans = [(at * HALF, size * HALF) for at, size in spans]
    for at, size in spans:
        first_layer(at, s_v, w1, b1, h1, size)
    ready_last(w3, b3, w3t, b3_rows)
    blocks = s_v.shape[1] // LANES
    per = HALF // LANES
    for block in range(max(begin * per - 1, 0), min(end * per + 1, blocks)):
        rate_at(block, s_v, w_v, deriv, rate, block)
    copies = []
    for at, size in spans:
        finish_tile(at, count, s_v, w2, b2, w3t, b3_rows, h1, h2, rate, o_v, size)
        cols = pl.ds(at, size)
        copies.append(pltpu.make_async_copy(o_v.at[:, cols], o_hbm.at[:, cols], sem))
        copies[-1].start()
    if begin == 0:
        held_ref[0] = o_v[:, 0:LANES]
    held_ref[1] = o_v[:, pl.ds(last_block(count), LANES)]
    for copy in copies:
        copy.wait()


def edge_kernel(live_ref, s_hbm, w_hbm, d_hbm, last_ref, s_e, w_e, deriv, sems):
    start = own_live(live_ref) - 16
    block = pl.multiple_of(start // LANES * LANES, LANES)
    copies = [
        fetch(s_hbm.at[:, pl.ds(block, LANES)], s_e, sems, 0),
        fetch(w_hbm.at[:, pl.ds(block, LANES)], w_e, sems, 1),
        fetch(d_hbm, deriv, sems, 2),
    ]
    for copy in copies:
        copy.wait()
    rate = block_rate(s_e[...], both_fields(w_e[0:64]), both_fields(w_e[64:128]), deriv[...])
    last_ref[...] = edge_of(rate, start - block + 3, 0)


def early_kernel(
    live_ref, last_ref, s_v, w_v, w1, b1, w2, b2, w3, b3, deriv, first_ref, held_ref, o_hbm,
    w3t, b3_rows, h1, h2, rate, o_v, sems,
):
    del last_ref
    rate_at(0, s_v, w_v, deriv, rate, 0)
    first_ref[...] = edge_of(rate[:, LANES : 2 * LANES], LANES - 3, 3)
    early = early_tiles()
    refs = [s_v, w1, b1, w2, b2, w3, b3, deriv, w_v, w3t, b3_rows, h1, h2, rate, o_v]
    for amount in sorted(set(EARLY[0] + EARLY[1]) - {0}):

        @pl.when(early == amount)
        def _():
            do_tiles(0, amount, own_live(live_ref), refs, held_ref, o_hbm, sems.at[0])


def late_kernel(
    live_ref, s_v, w_v, w1, b1, w2, b2, w3, b3, deriv, i_hbm, held_ref, o_hbm,
    w3t, b3_rows, h1, h2, rate, o_v, sems,
):
    del i_hbm
    early = early_tiles()
    refs = [s_v, w1, b1, w2, b2, w3, b3, deriv, w_v, w3t, b3_rows, h1, h2, rate, o_v]
    tiles = s_v.shape[1] // HALF
    for amount in sorted(set(EARLY[0] + EARLY[1]) | {0}):

        @pl.when(early == amount)
        def _():
            do_tiles(amount, tiles, own_live(live_ref), refs, held_ref, o_hbm, sems.at[0])


def twin_kernel(
    live_ref, after_ref, before_ref, early_ref, late_ref, i_hbm, o_hbm, held, sems
):
    del i_hbm
    count = own_live(live_ref)
    block = last_block(count)
    border = early_tiles() * HALF
    pad = jnp.zeros((LANES - 16, LANES), F32)
    half = 0.5 * TIMESTEP
    west = half * jnp.concatenate([before_ref[...], pad], axis=0).T
    east = half * pltpu.roll(
        jnp.concatenate([after_ref[...], pad], axis=0).T, count - 16 - block, 1
    )
    shared = block == 0
    begun = jnp.where(border > 0, early_ref[0], late_ref[0])
    ended = jnp.where(block < border, early_ref[1], late_ref[1])
    held[0] = begun + west + jnp.where(shared, east, 0.0)
    held[1] = ended + east
    stores = [
        pltpu.make_async_copy(held.at[0], o_hbm.at[:, pl.ds(0, LANES)], sems.at[0]),
        pltpu.make_async_copy(held.at[1], o_hbm.at[:, pl.ds(block, LANES)], sems.at[1]),
    ]
    stores[0].start()

    @pl.when(block > 0)
    def _():
        stores[1].start()
        stores[1].wait()

    stores[0].wait()


def passed_along(block, axis, distance):
    devices = range(lax.axis_size(axis))
    route = [((i - distance) % len(devices), i) for i in devices]
    return lax.ppermute(block, axis, route)


def body(state, wind, live, w_first, b_first, w_second, b_second, w_third, b_third):
    fields, levels, columns = state.shape
    features = fields * levels
    units = w_first.shape[1]
    s = state.reshape(features, columns)
    w = wind.reshape(features, columns)
    deriv = deriv_operand()
    smem = pl.BlockSpec(memory_space=pltpu.SMEM)
    vmem = pl.BlockSpec(memory_space=pltpu.VMEM)
    hbm = pl.BlockSpec(memory_space=pltpu.HBM)
    edge = jax.ShapeDtypeStruct((16, LANES), F32)
    whole = jax.ShapeDtypeStruct((features, columns), F32)
    operands = [
        s, w, w_first, b_first[None], w_second, b_second[None], w_third, b_third[None], deriv
    ]
    work = [
        pltpu.VMEM((LANES, units), BF),
        pltpu.VMEM((LANES, LANES), F32),
        pltpu.VMEM((columns, units), BF),
        pltpu.VMEM((TILE, units), BF),
        pltpu.VMEM((features, columns + 2 * LANES), F32),
        pltpu.VMEM((features, columns), F32),
    ]
    pair = pltpu.VMEM((2, features, LANES), F32)
    pair_out = jax.ShapeDtypeStruct((2, features, LANES), F32)
    block = pltpu.VMEM((features, LANES), F32)
    last = pl.pallas_call(
        edge_kernel,
        out_shape=edge,
        in_specs=[smem, hbm, hbm, hbm],
        out_specs=vmem,
        scratch_shapes=[block, block, pltpu.VMEM(deriv.shape, BF), pltpu.SemaphoreType.DMA((3,))],
        compiler_params=pltpu.CompilerParams(vmem_limit_bytes=54 * MIB - 128 * 1024),
        cost_estimate=pl.CostEstimate(flops=4 * 10**9, bytes_accessed=10**5, transcendentals=0),
    )(live, s, w, deriv)
    before = passed_along(last, ("grp", "col"), 1)
    work.append(pltpu.SemaphoreType.DMA((1,)))
    params = pltpu.CompilerParams(vmem_limit_bytes=28 * MIB)
    first, held, out = pl.pallas_call(
        early_kernel,
        out_shape=(edge, pair_out, whole),
        in_specs=[smem, vmem] + [vmem] * len(operands),
        out_specs=(vmem, vmem, hbm),
        scratch_shapes=work,
        compiler_params=params,
    )(live, last, *operands)
    after = passed_along(first, ("grp", "col"), -1)
    rest, out = pl.pallas_call(
        late_kernel,
        out_shape=(pair_out, whole),
        in_specs=[smem] + [vmem] * len(operands) + [hbm],
        out_specs=(vmem, hbm),
        scratch_shapes=work,
        input_output_aliases={1 + len(operands): 1},
        compiler_params=params,
        cost_estimate=pl.CostEstimate(
            flops=6 * 10**9, bytes_accessed=6 * 10**6, transcendentals=4 * 10**6
        ),
    )(live, *operands, out)
    out = pl.pallas_call(
        twin_kernel,
        out_shape=whole,
        in_specs=[smem] + [vmem] * 4 + [hbm],
        out_specs=hbm,
        scratch_shapes=[pair, pltpu.SemaphoreType.DMA((2,))],
        input_output_aliases={5: 0},
        compiler_params=pltpu.CompilerParams(vmem_limit_bytes=2 * MIB),
    )(live, after, before, held, rest, out)
    return out.reshape(fields, levels, columns)


def solution(mesh):
    return jax.shard_map(
        body,
        mesh=mesh,
        in_specs=(
            P(None, None, ("grp", "col")),
            P(None, None, ("grp", "col")),
            P("grp", None),
            P(),
            P(),
            P(),
            P(),
            P(),
            P(),
        ),
        out_specs=P(None, None, ("grp", "col")),
        check_vma=False,
    )
```

```python
import functools

import jax
import jax.numpy as jnp
import numpy as np
from jax import lax
from jax.experimental import pallas as pl
from jax.experimental.pallas import tpu as pltpu
from jax.sharding import PartitionSpec as P

TIMESTEP = 0.1
LANES = 128
TILE = 512
HALF = 256
EARLY = ((5, 5, 4, 2, 2, 1, 1, 0), (2, 2, 2, 1, 1, 0, 0, 0))
CHUNK = 256
BF = jnp.bfloat16
F32 = jnp.float32
MIB = 2**20


def gll_table():
    points = np.array([-1.0, -1.0 / np.sqrt(5.0), 1.0 / np.sqrt(5.0), 1.0])
    legendre = 0.5 * (5.0 * points**3 - 3.0 * points)
    deriv_table = np.zeros((4, 4))
    for i in range(4):
        for j in range(4):
            if i != j:
                deriv_table[i, j] = legendre[i] / (legendre[j] * (points[i] - points[j]))
    deriv_table[0, 0] = -3.0
    deriv_table[3, 3] = 3.0
    return deriv_table


def deriv_operand():
    deriv_table = gll_table()
    along_xi = np.kron(np.eye(8), np.kron(np.eye(4), deriv_table)).T
    along_eta = np.kron(np.eye(8), np.kron(deriv_table, np.eye(4))).T
    both = np.concatenate([along_xi, along_eta], axis=1).astype(np.float32)
    high = both.astype(jnp.bfloat16)
    low = (both - high.astype(np.float32)).astype(jnp.bfloat16)
    return jnp.asarray(np.concatenate([high, high, low], axis=0))


def block_rate(s, wind_xi, wind_eta, deriv):
    high = s.astype(BF)
    low = (s - high.astype(F32)).astype(BF)
    d = jnp.dot(
        jnp.concatenate([high, low, high], axis=1), deriv, preferred_element_type=F32
    )
    return -(wind_xi * d[:, :LANES] + wind_eta * d[:, LANES:])


def both_fields(w):
    return jnp.concatenate([w, w], axis=0)


def lane_ids():
    return lax.broadcasted_iota(jnp.int32, (LANES, LANES), 1)


def own_live(live_ref):
    return live_ref[0, lax.axis_index("col")] * 16


def early_tiles():
    col = lax.axis_index("col")
    amount = 0
    for z in range(8):
        here = jnp.where(col // 8 == 0, EARLY[0][z], EARLY[1][z])
        amount = jnp.where(col % 8 == z, here, amount)
    return amount


def fetch(source, target, sems, index):
    copy = pltpu.make_async_copy(source, target, sems.at[index])
    copy.start()
    return copy


def last_block(count):
    return pl.multiple_of((count - 16) // LANES * LANES, LANES)


def edge_of(rate, lanes_back, row):
    turn = jnp.where(lanes_back > 0, LANES - lanes_back, 0)
    turned = pltpu.roll(rate, turn, 1).T[0:16]
    rows = lax.broadcasted_iota(jnp.int32, (16, LANES), 0)
    return jnp.where(rows % 4 == row, turned, 0.0)


def first_layer(at, s_v, w1, b1, h1, size):
    units = h1.shape[1]
    x = s_v[:, at : at + size].astype(BF)
    for n in range(0, units, CHUNK):
        a = lax.dot_general(
            x, w1[:, n : n + CHUNK], (((0,), (0,)), ((), ())), preferred_element_type=F32
        )
        h1[at : at + size, n : n + CHUNK] = jax.nn.silu(a + b1[:, n : n + CHUNK]).astype(BF)


def rate_at(block, s_v, w_v, deriv, rate, slot):
    cols = pl.ds(pl.multiple_of(block * LANES, LANES), LANES)
    rate[:, pl.ds(pl.multiple_of(slot * LANES + LANES, LANES), LANES)] = block_rate(
        s_v[:, cols], both_fields(w_v[0:64, cols]), both_fields(w_v[64:128, cols]), deriv[...]
    )


def finish_tile(at, count, s_v, w2, b2, w3t, b3_rows, h1, h2, rate, o_v, size):
    units = h1.shape[1]
    h = h1[at : at + size, :]
    for n in range(0, units, CHUNK):
        a = jnp.dot(h, w2[:, n : n + CHUNK], preferred_element_type=F32)
        h2[0:size, n : n + CHUNK] = jax.nn.silu(a + b2[:, n : n + CHUNK]).astype(BF)
    third = lax.dot_general(
        w3t[...], h2[0:size], (((1,), (1,)), ((), ())), preferred_element_type=F32
    )
    lanes = lane_ids()
    for k in range(0, size, LANES):
        base = at + k
        own = rate[:, pl.ds(base + LANES, LANES)]
        after = rate[:, pl.ds(base + 2 * LANES, LANES)]
        prior = rate[:, pl.ds(base, LANES)]
        ids = lanes + base
        east = pltpu.roll(jnp.where(lanes < 13, after, own), LANES - 13, 1)
        west = pltpu.roll(jnp.where(lanes >= LANES - 13, prior, own), 13, 1)
        east = jnp.where(ids < count - 16, east, 0.0)
        west = jnp.where(ids >= 16, west, 0.0)
        twin = jnp.where(lanes % 4 == 3, east, jnp.where(lanes % 4 == 0, west, own))
        tendency = (third[:, k : k + LANES] + b3_rows[...]).astype(BF).astype(F32)
        value = s_v[:, pl.ds(base, LANES)] + (0.5 * TIMESTEP) * (own + twin) + tendency
        o_v[:, pl.ds(base, LANES)] = jnp.where(ids < count, value, 0.0)


def ready_last(w3, b3, w3t, b3_rows):
    w3t[...] = w3[...].T
    b3_rows[...] = jnp.broadcast_to(b3[...], (LANES, LANES)).T


def do_tiles(begin, end, count, refs, held_ref, o_hbm, sem):
    s_v, w1, b1, w2, b2, w3, b3, deriv, w_v, w3t, b3_rows, h1, h2, rate, o_v = refs
    spans = [(begin, 1)] if (end - begin) % 2 else []
    spans += [(at, 2) for at in range(begin + len(spans), end, 2)]
    spans = [(at * HALF, size * HALF) for at, size in spans]
    for at, size in spans:
        first_layer(at, s_v, w1, b1, h1, size)
    ready_last(w3, b3, w3t, b3_rows)
    blocks = s_v.shape[1] // LANES
    per = HALF // LANES
    for block in range(max(begin * per - 1, 0), min(end * per + 1, blocks)):
        rate_at(block, s_v, w_v, deriv, rate, block)
    copies = []
    for at, size in spans:
        finish_tile(at, count, s_v, w2, b2, w3t, b3_rows, h1, h2, rate, o_v, size)
        cols = pl.ds(at, size)
        copies.append(pltpu.make_async_copy(o_v.at[:, cols], o_hbm.at[:, cols], sem))
        copies[-1].start()
    if begin == 0:
        held_ref[0] = o_v[:, 0:LANES]
    held_ref[1] = o_v[:, pl.ds(last_block(count), LANES)]
    for copy in copies:
        copy.wait()


def edge_kernel(live_ref, s_hbm, w_hbm, d_hbm, last_ref, s_e, w_e, deriv, sems):
    start = own_live(live_ref) - 16
    block = pl.multiple_of(start // LANES * LANES, LANES)
    copies = [
        fetch(s_hbm.at[:, pl.ds(block, LANES)], s_e, sems, 0),
        fetch(w_hbm.at[:, pl.ds(block, LANES)], w_e, sems, 1),
        fetch(d_hbm, deriv, sems, 2),
    ]
    for copy in copies:
        copy.wait()
    rate = block_rate(s_e[...], both_fields(w_e[0:64]), both_fields(w_e[64:128]), deriv[...])
    last_ref[...] = edge_of(rate, start - block + 3, 0)


def early_kernel(
    live_ref, last_ref, s_v, w_v, w1, b1, w2, b2, w3, b3, deriv, first_ref, held_ref, o_hbm,
    w3t, b3_rows, h1, h2, rate, o_v, sems,
):
    del last_ref
    rate_at(0, s_v, w_v, deriv, rate, 0)
    first_ref[...] = edge_of(rate[:, LANES : 2 * LANES], LANES - 3, 3)
    early = early_tiles()
    refs = [s_v, w1, b1, w2, b2, w3, b3, deriv, w_v, w3t, b3_rows, h1, h2, rate, o_v]
    for amount in sorted(set(EARLY[0] + EARLY[1]) - {0}):

        @pl.when(early == amount)
        def _():
            do_tiles(0, amount, own_live(live_ref), refs, held_ref, o_hbm, sems.at[0])


def late_kernel(
    live_ref, s_v, w_v, w1, b1, w2, b2, w3, b3, deriv, i_hbm, held_ref, o_hbm,
    w3t, b3_rows, h1, h2, rate, o_v, sems,
):
    del i_hbm
    early = early_tiles()
    refs = [s_v, w1, b1, w2, b2, w3, b3, deriv, w_v, w3t, b3_rows, h1, h2, rate, o_v]
    tiles = s_v.shape[1] // HALF
    for amount in sorted(set(EARLY[0] + EARLY[1]) | {0}):

        @pl.when(early == amount)
        def _():
            do_tiles(amount, tiles, own_live(live_ref), refs, held_ref, o_hbm, sems.at[0])


def twin_kernel(
    live_ref, after_ref, before_ref, early_ref, late_ref, i_hbm, o_hbm, held, sems
):
    del i_hbm
    count = own_live(live_ref)
    block = last_block(count)
    border = early_tiles() * HALF
    pad = jnp.zeros((LANES - 16, LANES), F32)
    half = 0.5 * TIMESTEP
    west = half * jnp.concatenate([before_ref[...], pad], axis=0).T
    east = half * pltpu.roll(
        jnp.concatenate([after_ref[...], pad], axis=0).T, count - 16 - block, 1
    )
    shared = block == 0
    begun = jnp.where(border > 0, early_ref[0], late_ref[0])
    ended = jnp.where(block < border, early_ref[1], late_ref[1])
    held[0] = begun + west + jnp.where(shared, east, 0.0)
    held[1] = ended + east
    stores = [
        pltpu.make_async_copy(held.at[0], o_hbm.at[:, pl.ds(0, LANES)], sems.at[0]),
        pltpu.make_async_copy(held.at[1], o_hbm.at[:, pl.ds(block, LANES)], sems.at[1]),
    ]
    stores[0].start()

    @pl.when(block > 0)
    def _():
        stores[1].start()
        stores[1].wait()

    stores[0].wait()


def passed_along(block, axis, distance):
    devices = range(lax.axis_size(axis))
    route = [((i - distance) % len(devices), i) for i in devices]
    return lax.ppermute(block, axis, route)


def body(state, wind, live, w_first, b_first, w_second, b_second, w_third, b_third):
    fields, levels, columns = state.shape
    features = fields * levels
    units = w_first.shape[1]
    s = state.reshape(features, columns)
    w = wind.reshape(features, columns)
    deriv = deriv_operand()
    smem = pl.BlockSpec(memory_space=pltpu.SMEM)
    vmem = pl.BlockSpec(memory_space=pltpu.VMEM)
    hbm = pl.BlockSpec(memory_space=pltpu.HBM)
    edge = jax.ShapeDtypeStruct((16, LANES), F32)
    whole = jax.ShapeDtypeStruct((features, columns), F32)
    operands = [
        s, w, w_first, b_first[None], w_second, b_second[None], w_third, b_third[None], deriv
    ]
    work = [
        pltpu.VMEM((LANES, units), BF),
        pltpu.VMEM((LANES, LANES), F32),
        pltpu.VMEM((columns, units), BF),
        pltpu.VMEM((TILE, units), BF),
        pltpu.VMEM((features, columns + 2 * LANES), F32),
        pltpu.VMEM((features, columns), F32),
    ]
    pair = pltpu.VMEM((2, features, LANES), F32)
    pair_out = jax.ShapeDtypeStruct((2, features, LANES), F32)
    block = pltpu.VMEM((features, LANES), F32)
    last = pl.pallas_call(
        edge_kernel,
        out_shape=edge,
        in_specs=[smem, hbm, hbm, hbm],
        out_specs=vmem,
        scratch_shapes=[block, block, pltpu.VMEM(deriv.shape, BF), pltpu.SemaphoreType.DMA((3,))],
        compiler_params=pltpu.CompilerParams(vmem_limit_bytes=54 * MIB - 128 * 1024),
        cost_estimate=pl.CostEstimate(flops=4 * 10**9, bytes_accessed=10**5, transcendentals=0),
    )(live, s, w, deriv)
    before = passed_along(last, ("grp", "col"), 1)
    work.append(pltpu.SemaphoreType.DMA((1,)))
    params = pltpu.CompilerParams(vmem_limit_bytes=28 * MIB)
    first, held, out = pl.pallas_call(
        early_kernel,
        out_shape=(edge, pair_out, whole),
        in_specs=[smem, vmem] + [vmem] * len(operands),
        out_specs=(vmem, vmem, hbm),
        scratch_shapes=work,
        compiler_params=params,
    )(live, last, *operands)
    after = passed_along(first, ("grp", "col"), -1)
    rest, out = pl.pallas_call(
        late_kernel,
        out_shape=(pair_out, whole),
        in_specs=[smem] + [vmem] * len(operands) + [hbm],
        out_specs=(vmem, hbm),
        scratch_shapes=work,
        input_output_aliases={1 + len(operands): 1},
        compiler_params=params,
        cost_estimate=pl.CostEstimate(
            flops=6 * 10**9, bytes_accessed=6 * 10**6, transcendentals=4 * 10**6
        ),
    )(live, *operands, out)
    out = pl.pallas_call(
        twin_kernel,
        out_shape=whole,
        in_specs=[smem] + [vmem] * 4 + [hbm],
        out_specs=hbm,
        scratch_shapes=[pair, pltpu.SemaphoreType.DMA((2,))],
        input_output_aliases={5: 0},
        compiler_params=pltpu.CompilerParams(vmem_limit_bytes=2 * MIB),
    )(live, after, before, held, rest, out)
    return out.reshape(fields, levels, columns)


def solution(mesh):
    return jax.shard_map(
        body,
        mesh=mesh,
        in_specs=(
            P(None, None, ("grp", "col")),
            P(None, None, ("grp", "col")),
            P("grp", None),
            P(),
            P(),
            P(),
            P(),
            P(),
            P(),
        ),
        out_specs=P(None, None, ("grp", "col")),
        check_vma=False,
    )
```
